1024 devices in a mesh: table: 32 (over z), col: 4 (over y_lo, core), rep: 8 (over y_hi, x).
Axes of the slice: x: 4, y: 4 (y_hi: 2, y_lo: 2; y = y_hi * 2 + y_lo), z: 32, core: 2. Of those that a mesh axis runs over, the one named last changes fastest.
Arguments:
- pooled: bfloat16 [4096, 512, 160], P(('table', 'col', 'rep')), may hold values from -6 to 6
- upstream: bfloat16 [4096, 512, 160], P(('table', 'col', 'rep')), may hold values from -6 to 6
- lengths: int32 [4096, 512], P(('table', 'col', 'rep')), may hold values from 1 to 32
- w_lcb: bfloat16 [512, 512], replicated, may hold values from -0.25 to 0.25
- projection: bfloat16 [64, 512], replicated, may hold values from -0.25 to 0.25
- w_fmb: bfloat16 [64, 160], replicated, may hold values from -0.0625 to 0.0625
- feature_order: int32 [512], replicated, may hold values from 0 to 511, each once
- col_layout: int32 [32, 4], replicated, may hold values from 0 to 3, each once within a row
Outputs:
- table_grads: float32 [512, 4096, 160], P('table', 'rep', 'col')
- grad_lcb: float32 [512, 512], replicated
- grad_fmb: float32 [64, 160], replicated
- grad_proj: float32 [64, 512], replicated
The draws below stay inside these ranges and needn't reach their ends.
Inputs may be any that keep to these rules, and one draw needn't show every extreme that they name: `feature_order`: a permutation of the features. `col_layout`: each row is a permutation of the column shards.
All inputs are finite; a program needn't handle non-finite values. Where the reference program divides by a largest or mean magnitude, that divisor is 1e-20 or more.
Results may differ from the reference program's by a relative error of at most 0.012.
Values may be sent and summed in bfloat16 or wider, within the bound.
A program may use at most 32 MiB of HBM per device.

```python
import jax
import jax.numpy as jnp
from jax import lax

F = 512
D = 160
K = 64
SAMP_DEV = 4
SAMPLES = 4096
N_TABLE = 32
N_COL = 4
N_REP = 8


def set_ends(values, rng, low, largest):
    longest = values.shape.index(max(values.shape))
    spots = []
    for shift in (0, 1):
        where = [jax.random.randint(jax.random.fold_in(rng, axis), (), 0, length) for axis, length in enumerate(values.shape)]
        where[longest] = (where[longest] + shift) % values.shape[longest]
        spots.append(tuple(where))
    return values.at[spots[0]].set(low).at[spots[1]].set(largest)


def steps_of(own_key, dims, split, low, top_value):
    level, own = 1.0, jax.random.fold_in(own_key, 6)
    for dim, shards_of in split:
        heights = jnp.exp(jax.random.uniform(jax.random.fold_in(own, dim), (shards_of,), jnp.float32, low / len(split), top_value / len(split)))
        level = level * jnp.repeat(heights, dims[dim] // shards_of).reshape([-1 if axis == dim else 1 for axis in range(len(dims))])
    return level


def normal_values(stream_key, shape, spread, most, pieces=(), kind=jnp.bfloat16):
    array = jax.random.normal(stream_key, shape, jnp.float32) * spread
    if len(pieces) > 0:
        array = steps_of(stream_key, shape, pieces, -0.22, 0.18) * array
    return jnp.clip(array, min=-most, max=most).astype(kind)


def setup_inputs(seed: int = 0) -> dict:
    keys = jax.random.split(jax.random.key(seed), 9)
    return {
        "pooled": normal_values(keys[0], (SAMPLES, F, D), 1.0, 6.0, ((0, 1024),)),
        "upstream": normal_values(keys[1], (SAMPLES, F, D), 1.0, 6.0, ((0, 1024),)),
        "lengths": set_ends(jax.random.randint(keys[2], (SAMPLES, F), 1, 33), jax.random.fold_in(keys[2], 1), 1, 32).astype(jnp.int32),
        "w_lcb": normal_values(keys[3], (F, F), F ** -0.5, 0.25),
        "projection": normal_values(keys[4], (K, F), F ** -0.5, 0.25),
        "w_fmb": normal_values(keys[5], (K, D), (K * D) ** -0.5, 0.0625),
        "feature_order": jax.random.permutation(keys[6], F).astype(jnp.int32),
        "col_layout": jax.vmap(lambda own: jax.random.permutation(own, N_COL))(jax.random.split(keys[7], N_TABLE)).reshape((N_TABLE, N_COL)).astype(jnp.int32),
    }


def backward_block(pooled_wide, upstream_wide, length_block, lcb_wide, proj_wide, fmb_wide):
    highest = lax.Precision.HIGHEST
    compressed = jnp.einsum('kf,sfd->skd', proj_wide, pooled_wide, precision=highest).astype(jnp.bfloat16)
    compressed_wide = compressed.astype(jnp.float32)
    interact = jnp.einsum('sfd,skd->sfk', pooled_wide, compressed_wide, precision=highest).astype(jnp.bfloat16)
    grad_interact = jnp.einsum('sfd,kd->sfk', upstream_wide, fmb_wide, precision=highest).astype(jnp.bfloat16)
    interact_grad_wide = grad_interact.astype(jnp.float32)
    grad_compressed = jnp.einsum('sfk,sfd->skd', interact_grad_wide, pooled_wide, precision=highest).astype(jnp.bfloat16)
    compressed_grad_wide = grad_compressed.astype(jnp.float32)
    grad_input = upstream_wide + jnp.einsum('fg,sfd->sgd', lcb_wide, upstream_wide, precision=highest)
    grad_input = grad_input + jnp.einsum('sfk,skd->sfd', interact_grad_wide, compressed_wide, precision=highest)
    grad_input = grad_input + jnp.einsum('kf,skd->sfd', proj_wide, compressed_grad_wide, precision=highest)
    averaged = grad_input / length_block.astype(jnp.float32)[:, :, None]
    row_scale = (jnp.max(jnp.abs(averaged), axis=2) + 1e-6).astype(jnp.bfloat16)
    quantized = (averaged / row_scale.astype(jnp.float32)[:, :, None]).astype(jnp.bfloat16)
    grad_lcb = jnp.einsum('sfd,sgd->fg', upstream_wide, pooled_wide, precision=highest)
    grad_fmb = jnp.einsum('sfk,sfd->kd', interact.astype(jnp.float32), upstream_wide, precision=highest)
    grad_proj = jnp.einsum('skd,sfd->kf', compressed_grad_wide, pooled_wide, precision=highest)
    return quantized, row_scale, grad_lcb, grad_fmb, grad_proj


def reference(pooled, upstream, lengths, w_lcb, projection, w_fmb, feature_order, col_layout):
    sample_count = pooled.shape[0]
    features = pooled.shape[1]
    model_width = pooled.shape[2]
    block_count = sample_count // SAMP_DEV
    lcb_wide = w_lcb.astype(jnp.float32)
    proj_wide = projection.astype(jnp.float32)
    fmb_wide = w_fmb.astype(jnp.float32)

    def advance(totals, inputs):
        pooled_block, upstream_block, length_block = inputs
        quantized, row_scale, grad_lcb, grad_fmb, grad_proj = backward_block(
            pooled_block.astype(jnp.float32), upstream_block.astype(jnp.float32), length_block,
            lcb_wide, proj_wide, fmb_wide)
        totals = (totals[0] + grad_lcb, totals[1] + grad_fmb, totals[2] + grad_proj)
        return totals, (quantized, row_scale)

    start = (jnp.zeros((features, features), jnp.float32),
             jnp.zeros((K, model_width), jnp.float32),
             jnp.zeros((K, features), jnp.float32))
    totals, stacked = lax.scan(advance, start, (
        pooled.reshape(block_count, SAMP_DEV, features, model_width),
        upstream.reshape(block_count, SAMP_DEV, features, model_width),
        lengths.reshape(block_count, SAMP_DEV, features)))
    quantized = stacked[0].reshape(sample_count, features, model_width)
    row_scale = stacked[1].reshape(sample_count, features)
    restored = quantized.astype(jnp.float32) * row_scale.astype(jnp.float32)[:, :, None]
    restored = jnp.take(restored, feature_order, axis=1)
    group_rows = features // N_TABLE
    piece_width = model_width // N_COL
    restored = restored.reshape(sample_count, N_TABLE, group_rows, N_COL, piece_width)
    targets = jnp.arange(N_COL, dtype=jnp.int32)
    routing = (col_layout[:, None, :] == targets[None, :, None]).astype(jnp.int32)
    piece_of = jnp.sum(routing * targets[None, None, :], axis=2).astype(jnp.int32)
    index_full = jnp.broadcast_to(piece_of[None, :, None, :, None],
                                  (sample_count, N_TABLE, group_rows, N_COL, piece_width))
    placed = jnp.take_along_axis(restored, index_full, axis=3)
    placed = placed.reshape(N_TABLE, N_COL, N_REP, SAMP_DEV, N_TABLE, group_rows, N_COL, piece_width)
    placed = placed.transpose(4, 5, 2, 0, 1, 3, 6, 7).reshape(features, sample_count, model_width)
    return placed, totals[0], totals[1], totals[2]
```

```python
import jax
import jax.numpy as jnp
from jax import lax
from jax.experimental import pallas as pl
from jax.experimental.pallas import tpu as pltpu
from jax.sharding import PartitionSpec as P

MESH = pl.DeviceIdType.MESH
WIDE = jnp.float32
HALF = jnp.bfloat16
S = 4
F = 512
D = 160
K = 64
PIECE = 40
ROWS = 16
X = 640
NT = 32
NX = 32
BLOCK = 8
CHUNKS = 16
DEEP = 3
OWNERS = 5
APART = 6


def nn(a, b):
    return lax.dot_general(a, b, (((1,), (0,)), ((), ())), preferred_element_type=WIDE)


def nt(a, b):
    return lax.dot_general(a, b, (((1,), (1,)), ((), ())), preferred_element_type=WIDE)


def tn(a, b):
    return lax.dot_general(a, b, (((0,), (0,)), ((), ())), preferred_element_type=WIDE)


def one_hot(mask):
    return jnp.where(mask, 1.0, 0.0).astype(HALF)


def iota(shape, dim):
    return lax.broadcasted_iota(jnp.int32, shape, dim)


def kernel(
    x_ref, g_ref, len_ref, lcb_ref, proj_ref, fmb_ref, order_ref, lay_ref,
    out_ref, gw_ref,
    rst, wide, send, zbuf, msend, mrecv, ct, gct, git, part, wbuf, mine, zred, tiles, full, px,
    zs, zr, ms, mr, ws, wr, rs, rr, os, og, fs, fr,
):
    t = lax.axis_index("table")
    c = lax.axis_index("col")
    r = lax.axis_index("rep")
    me = c * 8 + r
    block = t // BLOCK
    within = lax.rem(t, BLOCK)

    def plane(k):
        return {"col": k // 8, "rep": lax.rem(k, 8)}

    def remote(src, dst, ss, rsem, device):
        return pltpu.make_async_remote_copy(
            src_ref=src, dst_ref=dst, send_sem=ss, recv_sem=rsem, device_id=device, device_id_type=MESH
        )

    def done(ref, sem):
        pltpu.make_async_copy(ref, ref, sem).wait()

    barrier = pltpu.get_barrier_semaphore()

    @pl.loop(1, NT)
    def _(d):
        pl.semaphore_signal(barrier, inc=1, device_id={"table": lax.rem(t + d, NT)}, device_id_type=MESH)

    @pl.loop(1, NX)
    def _(d):
        pl.semaphore_signal(barrier, inc=1, device_id=plane(lax.rem(me + d, NX)), device_id_type=MESH)

    proj = proj_ref[...]
    ct[...] = nt(x_ref[...], proj).astype(HALF)
    for i in range(S):
        rows = pl.ds(i * D, D)
        git[i] = nn(fmb_ref[...], g_ref[rows, :]).astype(HALF)
        gct[rows, :] = nt(x_ref[rows, :], git[i]).astype(HALF)
    for i in range(S):
        rows = pl.ds(i * D, D)
        g = g_ref[rows, :]
        grad = g.astype(WIDE) + nn(g, lcb_ref[...])
        grad = grad + nn(ct[rows, :], git[i])
        grad = grad + nn(gct[rows, :], proj)
        averaged = grad * (1.0 / len_ref[pl.ds(i, 1), :].astype(WIDE))
        largest = jnp.max(jnp.abs(averaged), axis=0, keepdims=True)
        scale = (largest + 1e-06).astype(HALF).astype(WIDE)
        quantized = (averaged * (1.0 / scale)).astype(HALF)
        rst[rows, :] = (quantized.astype(WIDE) * scale).astype(HALF)

    into = one_hot(iota((F, F), 0) == order_ref[...])
    for i in range(S):
        ordered = nn(rst[pl.ds(i * D, D), :], into)
        for j in range(4):
            for gb in range(4):
                wide[gb, pl.ds(i * 4 + j, PIECE, stride=ROWS), :] = ordered[
                    j * PIECE : (j + 1) * PIECE, gb * 128 : (gb + 1) * 128
                ]

    lane_block = iota((ROWS, 128), 1) // 16
    for eb in range(5):
        for gb in range(4):
            turned = []
            for e in range(8):
                tile = wide[gb, pl.ds((eb * 8 + e) * ROWS, ROWS), :]
                turned.append(pltpu.roll(tile, 16 * e, 1) if e else tile)
            for g in range(8):
                mixed = turned[0]
                for e in range(1, 8):
                    mixed = jnp.where(lane_block == (g + e) % 8, turned[e], mixed)
                send[gb * 8 + g, :, pl.ds(eb * 128, 128)] = mixed.astype(HALF)
    zbuf[t] = send[t]

    def along(m):
        side = m - 8
        q = jnp.where(m < 8, block + 2, jnp.where(m < 24, block + 1 + 2 * lax.rem(side, 2), block))
        d = jnp.where(m < 8, m, jnp.where(m < 24, side // 2, m - 23))
        return lax.rem(q, 4) * BLOCK + lax.rem(within + d, BLOCK)

    def start(m, q):
        p = along(m)
        remote(send.at[p], zbuf.at[t], zs.at[q], zr.at[block], {"table": p}).start()

    def issue(first, last):
        @pl.loop(first, last)
        def _(q):
            @pl.when(q >= DEEP)
            def _():
                done(send.at[pl.ds(0, 2)], zs.at[q - DEEP])

            start(2 * q, q)

            @pl.when(q < CHUNKS - 1)
            def _():
                start(2 * q + 1, q)

    pl.semaphore_wait(barrier, NT + NX - 2)
    issue(0, DEEP)

    fmb_part = jnp.zeros((D, K), WIDE)
    for i in range(S):
        rows = pl.ds(i * D, D)
        interact = tn(ct[rows, :], x_ref[rows, :]).astype(HALF)
        fmb_part = fmb_part + nt(g_ref[rows, :], interact)
    part[:, pl.ds(0, F)] = tn(g_ref[...], x_ref[...])
    proj_part = tn(x_ref[...], gct[...])
    pad = jnp.zeros((F - D, K), WIDE)
    part[:, pl.ds(F, 128)] = jnp.concatenate([proj_part, jnp.concatenate([fmb_part, pad], axis=0)], axis=1)

    @pl.loop(1, NX)
    def _(d):
        k = lax.rem(me + d, NX)
        rows = pl.ds(pl.multiple_of(k * ROWS, ROWS), ROWS)
        remote(part.at[rows, :], wbuf.at[me], ws, wr, plane(k)).start()

    wbuf[me] = part[pl.ds(pl.multiple_of(me * ROWS, ROWS), ROWS), :]

    e = iota((PIECE, X), 0)
    place = (e // 8) * 128 + lax.rem(lax.rem(e, 8) + lax.rem(t, 8), 8) * 16
    for h in range(ROWS):
        px[pl.ds(h * PIECE, PIECE), :] = one_hot(iota((PIECE, X), 1) == place + h)
    a = iota((128, 128), 0)
    b = iota((128, 128), 1)
    j = b % 4
    owner = jnp.where(
        j == 0, lay_ref[t, 0], jnp.where(j == 1, lay_ref[t, 1], jnp.where(j == 2, lay_ref[t, 2], lay_ref[t, 3]))
    )
    by_column = one_hot((a % 32 == b // 4) & (owner == a // 32))
    by_sample = one_hot(b == ((a // 4) % 4) * 32 + (a // 16) * 4 + a % 4)

    issue(DEEP, 9)

    done(wbuf.at[pl.ds(0, NX - 1)], wr)
    total = wbuf[0]
    for k in range(1, NX):
        total = total + wbuf[k]
    for o in range(OWNERS):
        mine[o] = total[:, o * 128 : (o + 1) * 128]
    turn = lax.rem(t - me + NT, NT)
    owns = (lax.rem(turn, APART) == 0) & (turn < OWNERS * APART)
    index = jnp.minimum(turn // APART, OWNERS - 1)

    for o in range(OWNERS):
        to = lax.rem(me + o * APART, NT)

        @pl.when(to != t)
        def _():
            remote(mine.at[o], zred.at[t], rs, rr, {"table": to}).start()

    zred[t] = mine[index]

    def batch(s):
        return lax.rem(block + s, 4)

    def gather(s, count):
        q = batch(s)
        done(zbuf.at[pl.ds(0, count)], zr.at[q])
        got = zbuf[pl.ds(pl.multiple_of(q * BLOCK, BLOCK), BLOCK)].reshape(128, X)
        msend[q] = nn(by_column, got).astype(HALF).reshape(4, 32, X)
        for d in range(1, 4):
            k = lax.rem(c + d, 4)
            remote(msend.at[q, k], mrecv.at[q, c], ms.at[q], mr.at[q], {"col": k}).start()
        mrecv[q, c] = msend[q, c]

    def finish(s):
        q = batch(s)
        done(mrecv.at[q, pl.ds(0, 3)], mr.at[q])
        got = nn(by_sample, mrecv[q].reshape(128, X)).astype(HALF)
        out_ref[:, pl.ds(pl.multiple_of(q * 128, 128), 128)] = nt(px[...], got)

    issue(9, 12)
    gather(2, BLOCK)
    issue(12, 13)

    @pl.when(owns)
    def _():
        done(zred.at[pl.ds(0, NT - 1)], rr)
        over = zred[0]
        for k in range(1, NT):
            over = over + zred[k]
        tiles[index] = over.astype(HALF)

        @pl.loop(1, NT)
        def _(d):
            remote(tiles.at[index], tiles.at[index], os, og, {"table": lax.rem(t + d, NT)}).start()

    issue(13, CHUNKS)
    finish(2)
    gather(1, BLOCK)
    gather(3, BLOCK)

    @pl.when(owns)
    def _():
        done(tiles.at[pl.ds(0, OWNERS - 1)], og)

    @pl.when(jnp.logical_not(owns))
    def _():
        done(tiles, og)

    @pl.loop(1, NX)
    def _(d):
        remote(tiles, full.at[me], fs, fr, plane(lax.rem(me + d, NX))).start()

    full[me] = tiles[...]
    finish(1)
    finish(3)
    gather(0, BLOCK - 1)
    finish(0)

    done(full.at[pl.ds(0, NX - 1)], fr)
    for k in range(NX):
        for o in range(OWNERS):
            gw_ref[pl.ds(k * ROWS, ROWS), pl.ds(o * 128, 128)] = full[k, o].astype(WIDE)

    for q in range(CHUNKS - DEEP, CHUNKS):
        done(send.at[pl.ds(0, 2 if q < CHUNKS - 1 else 1)], zs.at[q])
    for q in range(4):
        done(msend.at[q, pl.ds(0, 3)], ms.at[q])
    done(part.at[pl.ds(0, F - ROWS), :], ws)
    done(full.at[pl.ds(0, NX - 1)], fs)

    @pl.when(owns)
    def _():
        done(mine.at[pl.ds(0, OWNERS - 1)], rs)
        done(zbuf.at[pl.ds(0, NT - 1), :, pl.ds(0, 128)], os)

    @pl.when(jnp.logical_not(owns))
    def _():
        done(mine, rs)


def body(pooled, upstream, lengths, w_lcb, projection, w_fmb, feature_order, col_layout):
    x = pooled.transpose(0, 2, 1).reshape(S * D, F)
    g = upstream.transpose(0, 2, 1).reshape(S * D, F)
    vmem = pl.BlockSpec(memory_space=pltpu.VMEM)
    dma = pltpu.SemaphoreType.DMA
    out, gw = pl.pallas_call(
        kernel,
        out_shape=(jax.ShapeDtypeStruct((X, 512), WIDE), jax.ShapeDtypeStruct((F, X), WIDE)),
        in_specs=[vmem] * 7 + [pl.BlockSpec(memory_space=pltpu.SMEM)],
        out_specs=(vmem, vmem),
        scratch_shapes=[
            pltpu.VMEM((S * D, F), HALF),
            pltpu.VMEM((4, X, 128), WIDE),
            pltpu.VMEM((NT, ROWS, X), HALF),
            pltpu.VMEM((NT, ROWS, X), HALF),
            pltpu.VMEM((4, 4, 32, X), HALF),
            pltpu.VMEM((4, 4, 32, X), HALF),
            pltpu.VMEM((S * D, K), HALF),
            pltpu.VMEM((S * D, K), HALF),
            pltpu.VMEM((S, K, F), HALF),
            pltpu.VMEM((F, X), WIDE),
            pltpu.VMEM((NX, ROWS, X), WIDE),
            pltpu.VMEM((OWNERS, ROWS, 128), WIDE),
            pltpu.VMEM((NT, ROWS, 128), WIDE),
            pltpu.VMEM((OWNERS, ROWS, 128), HALF),
            pltpu.VMEM((NX, OWNERS, ROWS, 128), HALF),
            pltpu.VMEM((X, X), HALF),
            dma((CHUNKS,)), dma((4,)), dma((4,)), dma((4,)),
            dma, dma, dma, dma, dma, dma, dma, dma,
        ],
        compiler_params=pltpu.CompilerParams(
            collective_id=0, has_side_effects=True, vmem_limit_bytes=48 * 1024 * 1024
        ),
        cost_estimate=pl.CostEstimate(flops=2_500_000_000, bytes_accessed=6_000_000, transcendentals=0),
        name="interaction_backward",
    )(x, g, lengths, w_lcb, projection, w_fmb, feature_order.reshape(1, F), col_layout)
    table_grads = out.reshape(ROWS, PIECE, 512).transpose(0, 2, 1)
    return table_grads, gw[:, :F], gw[:D, F + K :].T, gw[:, F : F + K].T


def solution(mesh):
    placed = P(("table", "col", "rep"), None, None)
    return jax.shard_map(
        body,
        mesh=mesh,
        in_specs=(placed, placed, P(("table", "col", "rep"), None), P(), P(), P(), P(), P()),
        out_specs=(P("table", "rep", "col"), P(), P(), P()),
        check_vma=False,
    )
```

```python
import jax
import jax.numpy as jnp
from jax import lax
from jax.experimental import pallas as pl
from jax.experimental.pallas import tpu as pltpu
from jax.sharding import PartitionSpec as P

MESH = pl.DeviceIdType.MESH
WIDE = jnp.float32
HALF = jnp.bfloat16
S = 4
F = 512
D = 160
K = 64
PIECE = 40
ROWS = 16
X = 640
NT = 32
NX = 32
BATCH = 8
OWNERS = 5
APART = 7
RUN = 4


def nn(a, b):
    return lax.dot_general(a, b, (((1,), (0,)), ((), ())), preferred_element_type=WIDE)


def nt(a, b):
    return lax.dot_general(a, b, (((1,), (1,)), ((), ())), preferred_element_type=WIDE)


def tn(a, b):
    return lax.dot_general(a, b, (((0,), (0,)), ((), ())), preferred_element_type=WIDE)


def one_hot(mask):
    return jnp.where(mask, 1.0, 0.0).astype(HALF)


def iota(shape, dim):
    return lax.broadcasted_iota(jnp.int32, shape, dim)


def kernel(
    x_hbm, g_hbm, len_hbm, lcb_hbm, proj_hbm, fmb_hbm, order_hbm, lay_ref,
    rows_ref, full,
    x_ref, g_ref, len_ref, lcb_ref, proj_ref, fmb_ref, order_ref,
    rst, wide, send, zbuf, msend, mrecv, ct, gct, git, part, pbuf, wbuf, mine, zred, tiles,
    ins, zs, zr, ms, mr, ps, pr, ws, wr, rs, rr, os, og, hs, fs, fr,
):
    t = lax.axis_index("table")
    c = lax.axis_index("col")
    r = lax.axis_index("rep")
    me = c * 8 + r

    def plane(k):
        return {"col": k // 8, "rep": lax.rem(k, 8)}

    def remote(src, dst, ss, rsem, device):
        return pltpu.make_async_remote_copy(
            src_ref=src, dst_ref=dst, send_sem=ss, recv_sem=rsem, device_id=device, device_id_type=MESH
        )

    def done(ref, sem):
        pltpu.make_async_copy(ref, ref, sem).wait()

    arriving = [
        pltpu.make_async_copy(src, dst, ins.at[n])
        for n, (src, dst) in enumerate((
            (g_hbm, g_ref), (fmb_hbm, fmb_ref), (x_hbm, x_ref), (proj_hbm, proj_ref),
            (lcb_hbm, lcb_ref), (len_hbm, len_ref), (order_hbm, order_ref),
        ))
    ]
    for copy in arriving:
        copy.start()

    barrier = pltpu.get_barrier_semaphore()

    @pl.loop(1, NT)
    def _(d):
        pl.semaphore_signal(barrier, inc=1, device_id={"table": lax.rem(t + d, NT)}, device_id_type=MESH)

    @pl.loop(1, NX)
    def _(d):
        pl.semaphore_signal(barrier, inc=1, device_id=plane(lax.rem(me + d, NX)), device_id_type=MESH)

    for copy in arriving:
        copy.wait()

    proj = proj_ref[...]
    ct[...] = nt(x_ref[...], proj).astype(HALF)
    for i in range(S):
        rows = pl.ds(i * D, D)
        git[i] = nn(fmb_ref[...], g_ref[rows, :]).astype(HALF)
        gct[rows, :] = nt(x_ref[rows, :], git[i]).astype(HALF)
    for i in range(S):
        rows = pl.ds(i * D, D)
        g = g_ref[rows, :]
        grad = g.astype(WIDE) + nn(g, lcb_ref[...])
        grad = grad + nn(ct[rows, :], git[i])
        grad = grad + nn(gct[rows, :], proj)
        averaged = grad * (1.0 / len_ref[pl.ds(i, 1), :].astype(WIDE))
        largest = jnp.max(jnp.abs(averaged), axis=0, keepdims=True)
        scale = (largest + 1e-06).astype(HALF).astype(WIDE)
        quantized = (averaged * (1.0 / scale)).astype(HALF)
        rst[rows, :] = (quantized.astype(WIDE) * scale).astype(HALF)

    into = one_hot(iota((F, F), 0) == order_ref[...])
    for i in range(S):
        ordered = nn(rst[pl.ds(i * D, D), :], into)
        for j in range(4):
            for gb in range(4):
                wide[gb, pl.ds(i * 4 + j, PIECE, stride=ROWS), :] = ordered[
                    j * PIECE : (j + 1) * PIECE, gb * 128 : (gb + 1) * 128
                ]

    lane_block = iota((ROWS, 128), 1) // 16
    for eb in range(5):
        for gb in range(4):
            turned = []
            for e in range(8):
                tile = wide[gb, pl.ds((eb * 8 + e) * ROWS, ROWS), :]
                turned.append(pltpu.roll(tile, 16 * e, 1) if e else tile)
            for g in range(8):
                mixed = turned[0]
                for e in range(1, 8):
                    mixed = jnp.where(lane_block == (g + e) % 8, turned[e], mixed)
                send[gb * 8 + g, :, pl.ds(eb * 128, 128)] = mixed.astype(HALF)
    zbuf[t] = send[t]

    def distance(m):
        return (30 - m) // 2 + 1

    waited = [0]

    def issue(first, last, deep):
        def left(m):
            done(send.at[0], zs.at[m])

        early = max(waited[0], first - deep)
        pl.loop(waited[0], early)(left)

        @pl.loop(first, last)
        def _(m):
            pl.when(m >= early + deep)(lambda: left(m - deep))
            d = distance(m)
            p = lax.rem(t + jnp.where(lax.rem(m, 2) == 0, d, NT - d), NT)
            remote(send.at[p], zbuf.at[t], zs.at[m], zr.at[(m + 1) // BATCH], {"table": p}).start()

        waited[0] = max(early, last - deep)

    def source(n, u):
        low, high = (13, 20) if n == 0 else (13 - 4 * n, 17 - 4 * n)
        if n == 0:
            offset = 0 if u == 7 else 13 + u
        else:
            offset = low + u if u < 4 else NT - low - (u - 4)
        return lax.rem(t + offset, NT)


    fmb_part = jnp.zeros((D, K), WIDE)
    for i in range(S):
        rows = pl.ds(i * D, D)
        interact = tn(ct[rows, :], x_ref[rows, :]).astype(HALF)
        fmb_part = fmb_part + nt(g_ref[rows, :], interact)
    part[:, pl.ds(0, F)] = tn(g_ref[...], x_ref[...])
    proj_part = tn(x_ref[...], gct[...])
    pad = jnp.zeros((F - D, K), WIDE)
    part[:, pl.ds(F, 128)] = jnp.concatenate([proj_part, jnp.concatenate([fmb_part, pad], axis=0)], axis=1)

    pl.semaphore_wait(barrier, NT + NX - 2)
    issue(0, 9, 9)

    core = lax.rem(c, 2)
    for u in range(2):
        rows = pl.ds(pl.multiple_of((1 - core + 2 * u) * 128, 128), 128)
        remote(part.at[rows, :], pbuf.at[u], ps, pr, {"col": c + 1 - 2 * core}).start()

    def pair_sum():
        done(pbuf, pr)
        for u in range(2):
            rows = pl.ds(pl.multiple_of((core + 2 * u) * 128, 128), 128)
            part[rows, :] = part[rows, :] + pbuf[u]
        at = (c // 2) * 8 + r

        @pl.loop(1, NX // 2)
        def _(d):
            w = lax.rem(at + d, NX // 2)
            k = (core + 2 * (w // 8)) * 8 + lax.rem(w, 8)
            rows = pl.ds(pl.multiple_of(k * ROWS, ROWS), ROWS)
            remote(part.at[rows, :], wbuf.at[at], ws, wr, plane(k)).start()

        wbuf[at] = part[pl.ds(pl.multiple_of(me * ROWS, ROWS), ROWS), :]

    a = iota((128, 128), 0)
    b = iota((128, 128), 1)
    j = b % 4
    owner = jnp.where(
        j == 0, lay_ref[0, t], jnp.where(j == 1, lay_ref[1, t], jnp.where(j == 2, lay_ref[2, t], lay_ref[3, t]))
    )
    by_column = one_hot((a % 32 == b // 4) & (owner == a // 32))
    by_sample = one_hot(b == ((a // 4) % 4) * 32 + (a // 16) * 4 + a % 4)

    def gather(n):
        done(zbuf.at[pl.ds(0, 8 if n else 7)], zr.at[n])
        got = jnp.concatenate([zbuf[source(n, u)] for u in range(BATCH)], axis=0)
        msend[n] = nn(by_column, got).astype(HALF).reshape(4, 32, X)
        for d in range(1, 4):
            k = lax.rem(c + d, 4)
            remote(msend.at[n, k], mrecv.at[n, c], ms.at[n], mr.at[n], {"col": k}).start()
        mrecv[n, c] = msend[n, c]

    def finish(n):
        done(mrecv.at[n, pl.ds(0, 3)], mr.at[n])
        got = nn(by_sample, mrecv[n].reshape(128, X)).astype(HALF)
        for u in range(BATCH):
            rows_ref[source(n, u)] = got[u * ROWS : (u + 1) * ROWS, :]

    turn = lax.rem(t - me + NT, NT)
    owns = (lax.rem(turn, APART) == 0) & (turn < OWNERS * APART)
    index = jnp.minimum(turn // APART, OWNERS - 1)

    def plane_sum():
        done(wbuf.at[pl.ds(0, NX // 2 - 1)], wr)
        total = wbuf[0]
        for k in range(1, NX // 2):
            total = total + wbuf[k]
        for o in range(OWNERS):
            mine[o] = total[:, o * 128 : (o + 1) * 128]
        for o in range(OWNERS):
            to = lax.rem(me + o * APART, NT)

            @pl.when(to != t)
            def _():
                remote(mine.at[o], zred.at[t], rs, rr, {"table": to}).start()

        zred[t] = mine[index]

    def table_sum():
        @pl.when(owns)
        def _():
            done(zred.at[pl.ds(0, NT - 1)], rr)
            over = zred[0]
            for k in range(1, NT):
                over = over + zred[k]
            tiles[index] = over.astype(HALF)

            @pl.loop(1, NT // RUN + RUN - 1)
            def _(d):
                to = jnp.where(d < NT // RUN, d * RUN, d - NT // RUN + 1)
                remote(tiles.at[index], tiles.at[index], os, og.at[index], {"table": lax.rem(t + to, NT)}).start()

    def behind(o):
        return lax.rem(turn - o * APART + NT, NT)

    def first(o):
        return (lax.rem(behind(o), RUN) == 0) & (behind(o) > 0)

    def hand_on():
        for o in range(OWNERS):

            @pl.when(first(o))
            def _():
                done(tiles.at[o], og.at[o])
                for d in range(1, RUN):
                    remote(tiles.at[o], tiles.at[o], hs.at[o], og.at[o], {"table": lax.rem(t + d, NT)}).start()

    def round_plane():
        for o in range(OWNERS):

            @pl.when(lax.rem(behind(o), RUN) > 0)
            def _():
                done(tiles.at[o], og.at[o])

        @pl.loop(1, NX)
        def _(d):
            remote(tiles, full.at[me], fs, fr, plane(lax.rem(me + d, NX))).start()

        full[me] = tiles[...]

    pair_sum()
    plane_sum()
    issue(9, 18, 9)
    gather(0)
    table_sum()
    issue(18, 24, 7)
    finish(0)
    gather(1)
    hand_on()
    issue(24, 31, 6)
    finish(1)
    round_plane()
    gather(2)
    finish(2)
    gather(3)
    finish(3)

    done(full.at[pl.ds(0, NX - 1)], fr)
    for m in range(waited[0], 31):
        done(send.at[0], zs.at[m])
    for n in range(4):
        done(msend.at[n, pl.ds(0, 3)], ms.at[n])
    done(pbuf, ps)
    done(part.at[pl.ds(0, F // 2 - ROWS), :], ws)
    done(full.at[pl.ds(0, NX - 1)], fs)

    @pl.when(owns)
    def _():
        done(mine.at[pl.ds(0, OWNERS - 1)], rs)
        done(zbuf.at[pl.ds(0, NT // RUN + RUN - 2), :, pl.ds(0, 128)], os)

    @pl.when(jnp.logical_not(owns))
    def _():
        done(mine, rs)

    for o in range(OWNERS):

        @pl.when(first(o))
        def _():
            done(tiles.at[pl.ds(0, RUN - 1)], hs.at[o])


def place(rows_ref, full, out_ref, lcb_ref, fmb_ref, proj_ref):
    t = lax.axis_index("table")
    e = iota((PIECE, X), 0)
    spot = (e // 8) * 128 + lax.rem(lax.rem(e, 8) + lax.rem(t, 8), 8) * 16
    px = jnp.concatenate([one_hot(iota((PIECE, X), 1) == spot + h) for h in range(ROWS)], axis=0)
    out_ref[...] = nt(px, rows_ref[...])
    tail = []
    for k in range(NX):
        rows = pl.ds(k * ROWS, ROWS)
        for o in range(4):
            lcb_ref[rows, pl.ds(o * 128, 128)] = full[k, o].astype(WIDE)
        tail.append(full[k, 4].astype(WIDE))
    tail = jnp.concatenate(tail, axis=0).T
    proj_ref[...] = tail[:K, :]
    fmb_ref[...] = tail[K:, :D]


def body(pooled, upstream, lengths, w_lcb, projection, w_fmb, feature_order, col_layout):
    x = pooled.transpose(0, 2, 1).reshape(S * D, F)
    g = upstream.transpose(0, 2, 1).reshape(S * D, F)
    vmem = pl.BlockSpec(memory_space=pltpu.VMEM)
    hbm = pl.BlockSpec(memory_space=pl.ANY)
    dma = pltpu.SemaphoreType.DMA
    rows, full = pl.pallas_call(
        kernel,
        out_shape=(
            jax.ShapeDtypeStruct((NT, ROWS, X), HALF),
            jax.ShapeDtypeStruct((NX, OWNERS, ROWS, 128), HALF),
        ),
        in_specs=[hbm] * 7 + [pl.BlockSpec(memory_space=pltpu.SMEM)],
        out_specs=(vmem, vmem),
        scratch_shapes=[
            pltpu.VMEM((S * D, F), HALF),
            pltpu.VMEM((S * D, F), HALF),
            pltpu.VMEM((S, F), jnp.int32),
            pltpu.VMEM((F, F), HALF),
            pltpu.VMEM((K, F), HALF),
            pltpu.VMEM((K, D), HALF),
            pltpu.VMEM((1, F), jnp.int32),
            pltpu.VMEM((S * D, F), HALF),
            pltpu.VMEM((4, X, 128), WIDE),
            pltpu.VMEM((NT, ROWS, X), HALF),
            pltpu.VMEM((NT, ROWS, X), HALF),
            pltpu.VMEM((4, 4, 32, X), HALF),
            pltpu.VMEM((4, 4, 32, X), HALF),
            pltpu.VMEM((S * D, K), HALF),
            pltpu.VMEM((S * D, K), HALF),
            pltpu.VMEM((S, K, F), HALF),
            pltpu.VMEM((F, X), WIDE),
            pltpu.VMEM((2, 128, X), WIDE),
            pltpu.VMEM((NX // 2, ROWS, X), WIDE),
            pltpu.VMEM((OWNERS, ROWS, 128), WIDE),
            pltpu.VMEM((NT, ROWS, 128), WIDE),
            pltpu.VMEM((OWNERS, ROWS, 128), HALF),
            dma((7,)), dma((31,)), dma((4,)), dma((4,)), dma((4,)),
            dma, dma, dma, dma, dma, dma, dma, dma((OWNERS,)), dma((OWNERS,)), dma, dma,
        ],
        compiler_params=pltpu.CompilerParams(
            collective_id=0, has_side_effects=True, vmem_limit_bytes=56 * 1024 * 1024
        ),
        cost_estimate=pl.CostEstimate(flops=2_500_000_000, bytes_accessed=6_000_000, transcendentals=0),
        name="interaction_backward",
    )(x, g, lengths, w_lcb, projection, w_fmb, feature_order.reshape(1, F), col_layout.T)
    out, lcb, fmb, proj = pl.pallas_call(
        place,
        out_shape=(
            jax.ShapeDtypeStruct((X, 512), WIDE),
            jax.ShapeDtypeStruct((F, F), WIDE),
            jax.ShapeDtypeStruct((K, D), WIDE),
            jax.ShapeDtypeStruct((K, F), WIDE),
        ),
        in_specs=[vmem] * 2,
        out_specs=(vmem,) * 4,
        compiler_params=pltpu.CompilerParams(vmem_limit_bytes=32 * 1024 * 1024),
        name="place",
    )(rows.reshape(512, X), full)
    return out.reshape(ROWS, PIECE, 512).transpose(0, 2, 1), lcb, fmb, proj


def solution(mesh):
    placed = P(("table", "col", "rep"), None, None)
    return jax.shard_map(
        body,
        mesh=mesh,
        in_specs=(placed, placed, P(("table", "col", "rep"), None), P(), P(), P(), P(), P()),
        out_specs=(P("table", "rep", "col"), P(), P(), P()),
        check_vma=False,
    )
```

```python
import jax
import jax.numpy as jnp
from jax import lax
from jax.experimental import pallas as pl
from jax.experimental.pallas import tpu as pltpu
from jax.sharding import PartitionSpec as P

MESH = pl.DeviceIdType.MESH
WIDE = jnp.float32
HALF = jnp.bfloat16
S = 4
F = 512
D = 160
K = 64
PIECE = 40
ROWS = 16
X = 640
NT = 32
NX = 32
BATCH = (8, 8, 8, 4, 4)
OWNERS = 5
APART = 7
RUN = 4


def nn(a, b):
    return lax.dot_general(a, b, (((1,), (0,)), ((), ())), preferred_element_type=WIDE)


def nt(a, b):
    return lax.dot_general(a, b, (((1,), (1,)), ((), ())), preferred_element_type=WIDE)


def tn(a, b):
    return lax.dot_general(a, b, (((0,), (0,)), ((), ())), preferred_element_type=WIDE)


def one_hot(mask):
    return jnp.where(mask, 1.0, 0.0).astype(HALF)


def iota(shape, dim):
    return lax.broadcasted_iota(jnp.int32, shape, dim)


def kernel(
    x_hbm, g_hbm, len_hbm, lcb_hbm, proj_hbm, fmb_hbm, order_hbm, lay_ref,
    rows_ref, full,
    x_ref, g_ref, len_ref, lcb_ref, proj_ref, fmb_ref, order_ref,
    rst, wide, send, zbuf, msend, mrecv, ct, gct, git, part, pbuf, wbuf, mine, zred, tiles,
    ins, zs, zr, ms, mr, ps, pr, ws, wr, rs, rr, os, og, hs, fs, fr,
):
    t = lax.axis_index("table")
    c = lax.axis_index("col")
    r = lax.axis_index("rep")
    me = c * 8 + r

    def plane(k):
        return {"col": k // 8, "rep": lax.rem(k, 8)}

    def remote(src, dst, ss, rsem, device):
        return pltpu.make_async_remote_copy(
            src_ref=src, dst_ref=dst, send_sem=ss, recv_sem=rsem, device_id=device, device_id_type=MESH
        )

    def done(ref, sem):
        pltpu.make_async_copy(ref, ref, sem).wait()

    arriving = [
        pltpu.make_async_copy(src, dst, ins.at[n])
        for n, (src, dst) in enumerate((
            (g_hbm, g_ref), (fmb_hbm, fmb_ref), (x_hbm, x_ref), (proj_hbm, proj_ref),
            (lcb_hbm, lcb_ref), (len_hbm, len_ref), (order_hbm, order_ref),
        ))
    ]
    for copy in arriving:
        copy.start()

    barrier = pltpu.get_barrier_semaphore()

    @pl.loop(1, NT)
    def _(d):
        pl.semaphore_signal(barrier, inc=1, device_id={"table": lax.rem(t + d, NT)}, device_id_type=MESH)

    @pl.loop(1, NX)
    def _(d):
        pl.semaphore_signal(barrier, inc=1, device_id=plane(lax.rem(me + d, NX)), device_id_type=MESH)

    for copy in arriving:
        copy.wait()

    proj = proj_ref[...]
    ct[...] = nt(x_ref[...], proj).astype(HALF)
    for i in range(S):
        rows = pl.ds(i * D, D)
        git[i] = nn(fmb_ref[...], g_ref[rows, :]).astype(HALF)
        gct[rows, :] = nt(x_ref[rows, :], git[i]).astype(HALF)
    for i in range(S):
        rows = pl.ds(i * D, D)
        g = g_ref[rows, :]
        grad = g.astype(WIDE) + nn(g, lcb_ref[...])
        grad = grad + nn(ct[rows, :], git[i])
        grad = grad + nn(gct[rows, :], proj)
        averaged = grad * (1.0 / len_ref[pl.ds(i, 1), :].astype(WIDE))
        largest = jnp.max(jnp.abs(averaged), axis=0, keepdims=True)
        scale = (largest + 1e-06).astype(HALF).astype(WIDE)
        quantized = (averaged * (1.0 / scale)).astype(HALF)
        rst[rows, :] = (quantized.astype(WIDE) * scale).astype(HALF)

    into = one_hot(iota((F, F), 0) == order_ref[...])
    for i in range(S):
        ordered = nn(rst[pl.ds(i * D, D), :], into)
        for j in range(4):
            for gb in range(4):
                wide[gb, pl.ds(i * 4 + j, PIECE, stride=ROWS), :] = ordered[
                    j * PIECE : (j + 1) * PIECE, gb * 128 : (gb + 1) * 128
                ]

    lane_block = iota((ROWS, 128), 1) // 16
    for eb in range(5):
        for gb in range(4):
            turned = []
            for e in range(8):
                tile = wide[gb, pl.ds((eb * 8 + e) * ROWS, ROWS), :]
                turned.append(pltpu.roll(tile, 16 * e, 1) if e else tile)
            for g in range(8):
                mixed = turned[0]
                for e in range(1, 8):
                    mixed = jnp.where(lane_block == (g + e) % 8, turned[e], mixed)
                send[gb * 8 + g, :, pl.ds(eb * 128, 128)] = mixed.astype(HALF)
    zbuf[t] = send[t]

    def distance(m):
        return (30 - m) // 2 + 1

    waited = [0]

    def issue(first, last, deep):
        def left(m):
            done(send.at[0], zs.at[m])

        early = max(waited[0], first - deep)
        pl.loop(waited[0], early)(left)

        @pl.loop(first, last)
        def _(m):
            pl.when(m >= early + deep)(lambda: left(m - deep))
            d = distance(m)
            p = lax.rem(t + jnp.where(lax.rem(m, 2) == 0, d, NT - d), NT)
            remote(send.at[p], zbuf.at[t], zs.at[m], zr.at[(m + 1) // 8 + m // 27], {"table": p}).start()

        waited[0] = max(early, last - deep)

    def source(n, u):
        if n == 0:
            offset = 0 if u == 7 else 13 + u
        else:
            low = (13, 9, 5, 3, 1)[n]
            half = BATCH[n] // 2
            offset = low + u if u < half else NT - low - (u - half)
        return lax.rem(t + offset, NT)

    fmb_part = jnp.zeros((D, K), WIDE)
    for i in range(S):
        rows = pl.ds(i * D, D)
        interact = tn(ct[rows, :], x_ref[rows, :]).astype(HALF)
        fmb_part = fmb_part + nt(g_ref[rows, :], interact)
    part[:, pl.ds(0, F)] = tn(g_ref[...], x_ref[...])
    proj_part = tn(x_ref[...], gct[...])
    pad = jnp.zeros((F - D, K), WIDE)
    part[:, pl.ds(F, 128)] = jnp.concatenate([proj_part, jnp.concatenate([fmb_part, pad], axis=0)], axis=1)

    pl.semaphore_wait(barrier, NT + NX - 2)
    issue(0, 9, 9)

    core = lax.rem(c, 2)
    for u in range(2):
        rows = pl.ds(pl.multiple_of((1 - core + 2 * u) * 128, 128), 128)
        remote(part.at[rows, :], pbuf.at[u], ps, pr, {"col": c + 1 - 2 * core}).start()

    def pair_sum():
        done(pbuf, pr)
        for u in range(2):
            rows = pl.ds(pl.multiple_of((core + 2 * u) * 128, 128), 128)
            part[rows, :] = part[rows, :] + pbuf[u]
        at = (c // 2) * 8 + r

        @pl.loop(1, NX // 2)
        def _(d):
            w = lax.rem(at + d, NX // 2)
            k = (core + 2 * (w // 8)) * 8 + lax.rem(w, 8)
            rows = pl.ds(pl.multiple_of(k * ROWS, ROWS), ROWS)
            remote(part.at[rows, :], wbuf.at[at], ws, wr, plane(k)).start()

        wbuf[at] = part[pl.ds(pl.multiple_of(me * ROWS, ROWS), ROWS), :]

    def orders(size):
        a = iota((16 * size, 16 * size), 0)
        b = iota((16 * size, 16 * size), 1)
        j = b % 4
        owner = jnp.where(
            j == 0, lay_ref[0, t], jnp.where(j == 1, lay_ref[1, t], jnp.where(j == 2, lay_ref[2, t], lay_ref[3, t]))
        )
        by_column = one_hot((a % (4 * size) == b // 4) & (owner == a // (4 * size)))
        by_sample = one_hot(b == ((a // 4) % 4) * (4 * size) + (a // 16) * 4 + a % 4)
        return by_column, by_sample

    order = {size: orders(size) for size in sorted(set(BATCH))}

    def gather(n):
        size = BATCH[n]
        part_rows = pl.ds(0, 4 * size)
        done(zbuf.at[pl.ds(0, size if n else size - 1)], zr.at[n])
        got = jnp.concatenate([zbuf[source(n, u)] for u in range(size)], axis=0)
        msend[n, :, part_rows, :] = nn(order[size][0], got).astype(HALF).reshape(4, 4 * size, X)
        for d in range(1, 4):
            k = lax.rem(c + d, 4)
            remote(
                msend.at[n, k, part_rows, :], mrecv.at[n, c, part_rows, :], ms.at[n], mr.at[n], {"col": k}
            ).start()
        mrecv[n, c, part_rows, :] = msend[n, c, part_rows, :]

    def finish(n):
        size = BATCH[n]
        part_rows = pl.ds(0, 4 * size)
        done(mrecv.at[n, pl.ds(0, 3), part_rows, :], mr.at[n])
        got = nn(order[size][1], mrecv[n, :, part_rows, :].reshape(16 * size, X)).astype(HALF)
        for u in range(size):
            rows_ref[source(n, u)] = got[u * ROWS : (u + 1) * ROWS, :]

    turn = lax.rem(t - me + NT, NT)
    owns = (lax.rem(turn, APART) == 0) & (turn < OWNERS * APART)
    index = jnp.minimum(turn // APART, OWNERS - 1)

    def plane_sum():
        done(wbuf.at[pl.ds(0, NX // 2 - 1)], wr)
        total = wbuf[0]
        for k in range(1, NX // 2):
            total = total + wbuf[k]
        for o in range(OWNERS):
            mine[o] = total[:, o * 128 : (o + 1) * 128].astype(HALF)
        for o in range(OWNERS):
            to = lax.rem(me + o * APART, NT)

            @pl.when(to != t)
            def _():
                remote(mine.at[o], zred.at[t], rs, rr, {"table": to}).start()

        zred[t] = mine[index]

    def table_sum():
        @pl.when(owns)
        def _():
            done(zred.at[pl.ds(0, NT - 1)], rr)
            over = zred[0].astype(WIDE)
            for k in range(1, NT):
                over = over + zred[k].astype(WIDE)
            tiles[index] = over.astype(HALF)

            @pl.loop(1, NT // RUN + RUN - 1)
            def _(d):
                to = jnp.where(d < NT // RUN, d * RUN, d - NT // RUN + 1)
                remote(tiles.at[index], tiles.at[index], os, og.at[index], {"table": lax.rem(t + to, NT)}).start()

    def behind(o):
        return lax.rem(turn - o * APART + NT, NT)

    def first(o):
        return (lax.rem(behind(o), RUN) == 0) & (behind(o) > 0)

    def hand_on():
        for o in range(OWNERS):

            @pl.when(first(o))
            def _():
                done(tiles.at[o], og.at[o])
                for d in range(1, RUN):
                    remote(tiles.at[o], tiles.at[o], hs.at[o], og.at[o], {"table": lax.rem(t + d, NT)}).start()

    def round_plane():
        for o in range(OWNERS):

            @pl.when(lax.rem(behind(o), RUN) > 0)
            def _():
                done(tiles.at[o], og.at[o])

        @pl.loop(1, NX)
        def _(d):
            remote(tiles, full.at[me], fs, fr, plane(lax.rem(me + d, NX))).start()

        full[me] = tiles[...]

    pair_sum()
    plane_sum()
    issue(9, 20, 12)
    gather(0)
    table_sum()
    issue(20, 31, 12)
    finish(0)
    gather(1)
    hand_on()
    finish(1)
    gather(2)
    round_plane()
    finish(2)
    gather(3)
    finish(3)
    gather(4)
    finish(4)

    done(full.at[pl.ds(0, NX - 1)], fr)
    for m in range(waited[0], 31):
        done(send.at[0], zs.at[m])
    for n, size in enumerate(BATCH):
        done(msend.at[n, pl.ds(0, 3), pl.ds(0, 4 * size), :], ms.at[n])
    done(pbuf, ps)
    done(part.at[pl.ds(0, F // 2 - ROWS), :], ws)
    done(full.at[pl.ds(0, NX - 1)], fs)

    @pl.when(owns)
    def _():
        done(mine.at[pl.ds(0, OWNERS - 1)], rs)
        done(zbuf.at[pl.ds(0, NT // RUN + RUN - 2), :, pl.ds(0, 128)], os)

    @pl.when(jnp.logical_not(owns))
    def _():
        done(mine, rs)

    for o in range(OWNERS):

        @pl.when(first(o))
        def _():
            done(tiles.at[pl.ds(0, RUN - 1)], hs.at[o])


def place(rows_hbm, full_hbm, out_hbm, lcb_hbm, fmb_hbm, proj_hbm, rows, full, out, lcb, fmb, proj, ins, outs):
    fetch = [
        pltpu.make_async_copy(src, dst, ins.at[n])
        for n, (src, dst) in enumerate(((rows_hbm, rows), (full_hbm, full)))
    ]
    store = [
        pltpu.make_async_copy(src, dst, outs.at[n])
        for n, (src, dst) in enumerate(((out, out_hbm), (lcb, lcb_hbm), (fmb, fmb_hbm), (proj, proj_hbm)))
    ]
    for copy in fetch:
        copy.start()
    t = lax.axis_index("table")
    e = iota((PIECE, X), 0)
    spot = (e // 8) * 128 + lax.rem(lax.rem(e, 8) + lax.rem(t, 8), 8) * 16
    px = jnp.concatenate([one_hot(iota((PIECE, X), 1) == spot + h) for h in range(ROWS)], axis=0)
    fetch[0].wait()
    out[...] = nt(px, rows[...])
    store[0].start()
    fetch[1].wait()
    tail = []
    for k in range(NX):
        at = pl.ds(k * ROWS, ROWS)
        for o in range(4):
            lcb[at, pl.ds(o * 128, 128)] = full[k, o].astype(WIDE)
        tail.append(full[k, 4].astype(WIDE))
    store[1].start()
    tail = jnp.concatenate(tail, axis=0).T
    proj[...] = tail[:K, :]
    fmb[...] = tail[K:, :D]
    store[2].start()
    store[3].start()
    for copy in store:
        copy.wait()


def body(pooled, upstream, lengths, w_lcb, projection, w_fmb, feature_order, col_layout):
    x = pooled.transpose(0, 2, 1).reshape(S * D, F)
    g = upstream.transpose(0, 2, 1).reshape(S * D, F)
    vmem = pl.BlockSpec(memory_space=pltpu.VMEM)
    hbm = pl.BlockSpec(memory_space=pl.ANY)
    dma = pltpu.SemaphoreType.DMA
    rows, full = pl.pallas_call(
        kernel,
        out_shape=(
            jax.ShapeDtypeStruct((NT, ROWS, X), HALF),
            jax.ShapeDtypeStruct((NX, OWNERS, ROWS, 128), HALF),
        ),
        in_specs=[hbm] * 7 + [pl.BlockSpec(memory_space=pltpu.SMEM)],
        out_specs=(vmem, vmem),
        scratch_shapes=[
            pltpu.VMEM((S * D, F), HALF),
            pltpu.VMEM((S * D, F), HALF),
            pltpu.VMEM((S, F), jnp.int32),
            pltpu.VMEM((F, F), HALF),
            pltpu.VMEM((K, F), HALF),
            pltpu.VMEM((K, D), HALF),
            pltpu.VMEM((1, F), jnp.int32),
            pltpu.VMEM((S * D, F), HALF),
            pltpu.VMEM((4, X, 128), WIDE),
            pltpu.VMEM((NT, ROWS, X), HALF),
            pltpu.VMEM((NT, ROWS, X), HALF),
            pltpu.VMEM((len(BATCH), 4, 32, X), HALF),
            pltpu.VMEM((len(BATCH), 4, 32, X), HALF),
            pltpu.VMEM((S * D, K), HALF),
            pltpu.VMEM((S * D, K), HALF),
            pltpu.VMEM((S, K, F), HALF),
            pltpu.VMEM((F, X), WIDE),
            pltpu.VMEM((2, 128, X), WIDE),
            pltpu.VMEM((NX // 2, ROWS, X), WIDE),
            pltpu.VMEM((OWNERS, ROWS, 128), HALF),
            pltpu.VMEM((NT, ROWS, 128), HALF),
            pltpu.VMEM((OWNERS, ROWS, 128), HALF),
            dma((7,)), dma((31,)), dma((len(BATCH),)), dma((len(BATCH),)), dma((len(BATCH),)),
            dma, dma, dma, dma, dma, dma, dma, dma((OWNERS,)), dma((OWNERS,)), dma, dma,
        ],
        compiler_params=pltpu.CompilerParams(
            collective_id=0, has_side_effects=True, vmem_limit_bytes=56 * 1024 * 1024
        ),
        cost_estimate=pl.CostEstimate(flops=2_500_000_000, bytes_accessed=6_000_000, transcendentals=0),
        name="interaction_backward",
    )(x, g, lengths, w_lcb, projection, w_fmb, feature_order.reshape(1, F), col_layout.T)
    out, lcb, fmb, proj = pl.pallas_call(
        place,
        out_shape=(
            jax.ShapeDtypeStruct((X, 512), WIDE),
            jax.ShapeDtypeStruct((F, F), WIDE),
            jax.ShapeDtypeStruct((K, D), WIDE),
            jax.ShapeDtypeStruct((K, F), WIDE),
        ),
        in_specs=[hbm] * 2,
        out_specs=(hbm,) * 4,
        scratch_shapes=[
            pltpu.VMEM((512, X), HALF),
            pltpu.VMEM((NX, OWNERS, ROWS, 128), HALF),
            pltpu.VMEM((X, 512), WIDE),
            pltpu.VMEM((F, F), WIDE),
            pltpu.VMEM((K, D), WIDE),
            pltpu.VMEM((K, F), WIDE),
            dma((2,)), dma((4,)),
        ],
        compiler_params=pltpu.CompilerParams(vmem_limit_bytes=56 * 1024 * 1024),
        name="place",
    )(rows.reshape(512, X), full)
    return out.reshape(ROWS, PIECE, 512).transpose(0, 2, 1), lcb, fmb, proj


def solution(mesh):
    placed = P(("table", "col", "rep"), None, None)
    return jax.shard_map(
        body,
        mesh=mesh,
        in_specs=(placed, placed, P(("table", "col", "rep"), None), P(), P(), P(), P(), P()),
        out_specs=(P("table", "rep", "col"), P(), P(), P()),
        check_vma=False,
    )
```

```python
import jax
import jax.numpy as jnp
from jax import lax
from jax.experimental import pallas as pl
from jax.experimental.pallas import tpu as pltpu
from jax.sharding import PartitionSpec as P

MESH = pl.DeviceIdType.MESH
WIDE = jnp.float32
HALF = jnp.bfloat16
S = 4
F = 512
D = 160
K = 64
PIECE = 40
ROWS = 16
X = 640
NT = 32
NX = 32
BATCH = (8, 8, 8, 4, 4)
OWNERS = 5
APART = 7
RUN = 4


def nn(a, b):
    return lax.dot_general(a, b, (((1,), (0,)), ((), ())), preferred_element_type=WIDE)


def nt(a, b):
    return lax.dot_general(a, b, (((1,), (1,)), ((), ())), preferred_element_type=WIDE)


def tn(a, b):
    return lax.dot_general(a, b, (((0,), (0,)), ((), ())), preferred_element_type=WIDE)


def one_hot(mask):
    return jnp.where(mask, 1.0, 0.0).astype(HALF)


def iota(shape, dim):
    return lax.broadcasted_iota(jnp.int32, shape, dim)


def kernel(
    x_hbm, g_hbm, len_hbm, lcb_hbm, proj_hbm, fmb_hbm, order_hbm, lay_ref,
    rows_ref, full,
    x_ref, g_ref, len_ref, lcb_ref, proj_ref, fmb_ref, order_ref,
    rst, wide, send, zbuf, msend, mrecv, ct, gct, git, part, pbuf, wbuf, mine, zred, tiles,
    ins, zs, zr, ms, mr, ps, pr, ws, wr, rs, rr, os, og, hs, fs, fr,
):
    t = lax.axis_index("table")
    c = lax.axis_index("col")
    r = lax.axis_index("rep")
    me = c * 8 + r

    def plane(k):
        return {"col": k // 8, "rep": lax.rem(k, 8)}

    def remote(src, dst, ss, rsem, device):
        return pltpu.make_async_remote_copy(
            src_ref=src, dst_ref=dst, send_sem=ss, recv_sem=rsem, device_id=device, device_id_type=MESH
        )

    def done(ref, sem):
        pltpu.make_async_copy(ref, ref, sem).wait()

    arriving = [
        pltpu.make_async_copy(src, dst, ins.at[n])
        for n, (src, dst) in enumerate((
            (g_hbm, g_ref), (fmb_hbm, fmb_ref), (x_hbm, x_ref), (proj_hbm, proj_ref),
            (lcb_hbm, lcb_ref), (len_hbm, len_ref), (order_hbm, order_ref),
        ))
    ]
    for copy in arriving:
        copy.start()

    barrier = pltpu.get_barrier_semaphore()

    @pl.loop(1, NT)
    def _(d):
        pl.semaphore_signal(barrier, inc=1, device_id={"table": lax.rem(t + d, NT)}, device_id_type=MESH)

    @pl.loop(1, NX)
    def _(d):
        pl.semaphore_signal(barrier, inc=1, device_id=plane(lax.rem(me + d, NX)), device_id_type=MESH)

    for copy in arriving:
        copy.wait()

    proj = proj_ref[...]
    ct[...] = nt(x_ref[...], proj).astype(HALF)
    for i in range(S):
        rows = pl.ds(i * D, D)
        git[i] = nn(fmb_ref[...], g_ref[rows, :]).astype(HALF)
        gct[rows, :] = nt(x_ref[rows, :], git[i]).astype(HALF)
    for i in range(S):
        rows = pl.ds(i * D, D)
        g = g_ref[rows, :]
        grad = g.astype(WIDE) + nn(g, lcb_ref[...])
        grad = grad + nn(ct[rows, :], git[i])
        grad = grad + nn(gct[rows, :], proj)
        averaged = grad * (1.0 / len_ref[pl.ds(i, 1), :].astype(WIDE))
        largest = jnp.max(jnp.abs(averaged), axis=0, keepdims=True)
        scale = (largest + 1e-06).astype(HALF).astype(WIDE)
        quantized = (averaged * (1.0 / scale)).astype(HALF)
        rst[rows, :] = (quantized.astype(WIDE) * scale).astype(HALF)

    into = one_hot(iota((F, F), 0) == order_ref[...])
    for i in range(S):
        ordered = nn(rst[pl.ds(i * D, D), :], into)
        for j in range(4):
            for gb in range(4):
                wide[gb, pl.ds(i * 4 + j, PIECE, stride=ROWS), :] = ordered[
                    j * PIECE : (j + 1) * PIECE, gb * 128 : (gb + 1) * 128
                ]

    lane_block = iota((ROWS, 128), 1) // 16
    for eb in range(5):
        for gb in range(4):
            turned = []
            for e in range(8):
                tile = wide[gb, pl.ds((eb * 8 + e) * ROWS, ROWS), :]
                turned.append(pltpu.roll(tile, 16 * e, 1) if e else tile)
            for g in range(8):
                mixed = turned[0]
                for e in range(1, 8):
                    mixed = jnp.where(lane_block == (g + e) % 8, turned[e], mixed)
                send[gb * 8 + g, :, pl.ds(eb * 128, 128)] = mixed.astype(HALF)
    zbuf[t] = send[t]

    def distance(m):
        return (30 - m) // 2 + 1

    waited = [0]

    def issue(first, last, deep):
        def left(m):
            done(send.at[0], zs.at[m])

        early = max(waited[0], first - deep)
        pl.loop(waited[0], early)(left)

        @pl.loop(first, last)
        def _(m):
            pl.when(m >= early + deep)(lambda: left(m - deep))
            d = distance(m)
            p = lax.rem(t + jnp.where(lax.rem(m, 2) == 0, d, NT - d), NT)
            remote(send.at[p], zbuf.at[t], zs.at[m], zr.at[(m + 1) // 8 + m // 27], {"table": p}).start()

        waited[0] = max(early, last - deep)

    def source(n, u):
        if n == 0:
            offset = 0 if u == 7 else 13 + u
        else:
            low = (13, 9, 5, 3, 1)[n]
            half = BATCH[n] // 2
            offset = low + u if u < half else NT - low - (u - half)
        return lax.rem(t + offset, NT)

    fmb_part = jnp.zeros((D, K), WIDE)
    for i in range(S):
        rows = pl.ds(i * D, D)
        interact = tn(ct[rows, :], x_ref[rows, :]).astype(HALF)
        fmb_part = fmb_part + nt(g_ref[rows, :], interact)
    part[:, pl.ds(0, F)] = tn(g_ref[...], x_ref[...])
    proj_part = tn(x_ref[...], gct[...])
    pad = jnp.zeros((F - D, K), WIDE)
    part[:, pl.ds(F, 128)] = jnp.concatenate([proj_part, jnp.concatenate([fmb_part, pad], axis=0)], axis=1)

    pl.semaphore_wait(barrier, NT + NX - 2)
    issue(0, 7, 7)

    core = lax.rem(c, 2)
    for u in range(2):
        rows = pl.ds(pl.multiple_of((1 - core + 2 * u) * 128, 128), 128)
        remote(part.at[rows, :], pbuf.at[u], ps, pr, {"col": c + 1 - 2 * core}).start()

    def pair_sum():
        done(pbuf, pr)
        for u in range(2):
            rows = pl.ds(pl.multiple_of((core + 2 * u) * 128, 128), 128)
            part[rows, :] = part[rows, :] + pbuf[u]
        at = (c // 2) * 8 + r

        @pl.loop(1, NX // 2)
        def _(d):
            w = lax.rem(at + d, NX // 2)
            k = (core + 2 * (w // 8)) * 8 + lax.rem(w, 8)
            rows = pl.ds(pl.multiple_of(k * ROWS, ROWS), ROWS)
            remote(part.at[rows, :], wbuf.at[at], ws, wr, plane(k)).start()

        wbuf[at] = part[pl.ds(pl.multiple_of(me * ROWS, ROWS), ROWS), :]

    def orders(size):
        a = iota((16 * size, 16 * size), 0)
        b = iota((16 * size, 16 * size), 1)
        j = b % 4
        owner = jnp.where(
            j == 0, lay_ref[0, t], jnp.where(j == 1, lay_ref[1, t], jnp.where(j == 2, lay_ref[2, t], lay_ref[3, t]))
        )
        by_column = one_hot((a % (4 * size) == b // 4) & (owner == a // (4 * size)))
        by_sample = one_hot(b == ((a // 4) % 4) * (4 * size) + (a // 16) * 4 + a % 4)
        return by_column, by_sample

    order = {size: orders(size) for size in sorted(set(BATCH))}

    def gather(n):
        size = BATCH[n]
        part_rows = pl.ds(0, 4 * size)
        done(zbuf.at[pl.ds(0, size if n else size - 1)], zr.at[n])
        got = jnp.concatenate([zbuf[source(n, u)] for u in range(size)], axis=0)
        msend[n, :, part_rows, :] = nn(order[size][0], got).astype(HALF).reshape(4, 4 * size, X)
        for d in range(1, 4):
            k = lax.rem(c + d, 4)
            remote(
                msend.at[n, k, part_rows, :], mrecv.at[n, c, part_rows, :], ms.at[n], mr.at[n], {"col": k}
            ).start()
        mrecv[n, c, part_rows, :] = msend[n, c, part_rows, :]

    def finish(n):
        size = BATCH[n]
        part_rows = pl.ds(0, 4 * size)
        done(mrecv.at[n, pl.ds(0, 3), part_rows, :], mr.at[n])
        got = nn(order[size][1], mrecv[n, :, part_rows, :].reshape(16 * size, X)).astype(HALF)
        for u in range(size):
            rows_ref[source(n, u)] = got[u * ROWS : (u + 1) * ROWS, :]

    turn = lax.rem(t - me + NT, NT)
    owns = (lax.rem(turn, APART) == 0) & (turn < OWNERS * APART)
    index = jnp.minimum(turn // APART, OWNERS - 1)

    def plane_sum():
        done(wbuf.at[pl.ds(0, NX // 2 - 1)], wr)
        total = wbuf[0]
        for k in range(1, NX // 2):
            total = total + wbuf[k]
        for o in range(OWNERS):
            mine[o] = total[:, o * 128 : (o + 1) * 128].astype(HALF)
        for o in range(OWNERS):
            to = lax.rem(me + o * APART, NT)

            @pl.when(to != t)
            def _():
                remote(mine.at[o], zred.at[t], rs, rr, {"table": to}).start()

        zred[t] = mine[index]

    def table_sum():
        @pl.when(owns)
        def _():
            done(zred.at[pl.ds(0, NT - 1)], rr)
            over = zred[0].astype(WIDE)
            for k in range(1, NT):
                over = over + zred[k].astype(WIDE)
            tiles[index] = over.astype(HALF)

            @pl.loop(1, NT // RUN + RUN - 1)
            def _(d):
                to = jnp.where(d < NT // RUN, d * RUN, d - NT // RUN + 1)
                remote(tiles.at[index], tiles.at[index], os, og.at[index], {"table": lax.rem(t + to, NT)}).start()

    def behind(o):
        return lax.rem(turn - o * APART + NT, NT)

    def first(o):
        return (lax.rem(behind(o), RUN) == 0) & (behind(o) > 0)

    def hand_on():
        for o in range(OWNERS):

            @pl.when(first(o))
            def _():
                done(tiles.at[o], og.at[o])
                for d in range(1, RUN):
                    remote(tiles.at[o], tiles.at[o], hs.at[o], og.at[o], {"table": lax.rem(t + d, NT)}).start()

    def round_plane():
        for o in range(OWNERS):

            @pl.when(lax.rem(behind(o), RUN) > 0)
            def _():
                done(tiles.at[o], og.at[o])

        @pl.loop(1, NX)
        def _(d):
            remote(tiles, full.at[me], fs, fr, plane(lax.rem(me + d, NX))).start()

        full[me] = tiles[...]

    pair_sum()
    plane_sum()
    issue(7, 17, 12)
    gather(0)
    table_sum()
    issue(17, 31, 10)
    finish(0)
    gather(1)
    hand_on()
    finish(1)
    gather(2)
    round_plane()
    finish(2)
    gather(3)
    finish(3)
    gather(4)
    finish(4)

    done(full.at[pl.ds(0, NX - 1)], fr)
    for m in range(waited[0], 31):
        done(send.at[0], zs.at[m])
    for n, size in enumerate(BATCH):
        done(msend.at[n, pl.ds(0, 3), pl.ds(0, 4 * size), :], ms.at[n])
    done(pbuf, ps)
    done(part.at[pl.ds(0, F // 2 - ROWS), :], ws)
    done(full.at[pl.ds(0, NX - 1)], fs)

    @pl.when(owns)
    def _():
        done(mine.at[pl.ds(0, OWNERS - 1)], rs)
        done(zbuf.at[pl.ds(0, NT // RUN + RUN - 2), :, pl.ds(0, 128)], os)

    @pl.when(jnp.logical_not(owns))
    def _():
        done(mine, rs)

    for o in range(OWNERS):

        @pl.when(first(o))
        def _():
            done(tiles.at[pl.ds(0, RUN - 1)], hs.at[o])


def place(rows_hbm, full_hbm, out_hbm, lcb_hbm, fmb_hbm, proj_hbm, rows, full, out, lcb, fmb, proj, ins, outs):
    fetch = [
        pltpu.make_async_copy(src, dst, ins.at[n])
        for n, (src, dst) in enumerate(((rows_hbm, rows), (full_hbm, full)))
    ]
    store = [
        pltpu.make_async_copy(src, dst, outs.at[n])
        for n, (src, dst) in enumerate(((out, out_hbm), (lcb, lcb_hbm), (fmb, fmb_hbm), (proj, proj_hbm)))
    ]
    for copy in fetch:
        copy.start()
    t = lax.axis_index("table")
    e = iota((PIECE, X), 0)
    spot = (e // 8) * 128 + lax.rem(lax.rem(e, 8) + lax.rem(t, 8), 8) * 16
    px = jnp.concatenate([one_hot(iota((PIECE, X), 1) == spot + h) for h in range(ROWS)], axis=0)
    fetch[0].wait()
    out[...] = nt(px, rows[...])
    store[0].start()
    fetch[1].wait()
    tail = []
    for k in range(NX):
        at = pl.ds(k * ROWS, ROWS)
        for o in range(4):
            lcb[at, pl.ds(o * 128, 128)] = full[k, o].astype(WIDE)
        tail.append(full[k, 4].astype(WIDE))
    store[1].start()
    tail = jnp.concatenate(tail, axis=0).T
    proj[...] = tail[:K, :]
    fmb[...] = tail[K:, :D]
    store[2].start()
    store[3].start()
    for copy in store:
        copy.wait()


def body(pooled, upstream, lengths, w_lcb, projection, w_fmb, feature_order, col_layout):
    x = pooled.transpose(0, 2, 1).reshape(S * D, F)
    g = upstream.transpose(0, 2, 1).reshape(S * D, F)
    vmem = pl.BlockSpec(memory_space=pltpu.VMEM)
    hbm = pl.BlockSpec(memory_space=pl.ANY)
    dma = pltpu.SemaphoreType.DMA
    rows, full = pl.pallas_call(
        kernel,
        out_shape=(
            jax.ShapeDtypeStruct((NT, ROWS, X), HALF),
            jax.ShapeDtypeStruct((NX, OWNERS, ROWS, 128), HALF),
        ),
        in_specs=[hbm] * 7 + [pl.BlockSpec(memory_space=pltpu.SMEM)],
        out_specs=(vmem, vmem),
        scratch_shapes=[
            pltpu.VMEM((S * D, F), HALF),
            pltpu.VMEM((S * D, F), HALF),
            pltpu.VMEM((S, F), jnp.int32),
            pltpu.VMEM((F, F), HALF),
            pltpu.VMEM((K, F), HALF),
            pltpu.VMEM((K, D), HALF),
            pltpu.VMEM((1, F), jnp.int32),
            pltpu.VMEM((S * D, F), HALF),
            pltpu.VMEM((4, X, 128), WIDE),
            pltpu.VMEM((NT, ROWS, X), HALF),
            pltpu.VMEM((NT, ROWS, X), HALF),
            pltpu.VMEM((len(BATCH), 4, 32, X), HALF),
            pltpu.VMEM((len(BATCH), 4, 32, X), HALF),
            pltpu.VMEM((S * D, K), HALF),
            pltpu.VMEM((S * D, K), HALF),
            pltpu.VMEM((S, K, F), HALF),
            pltpu.VMEM((F, X), WIDE),
            pltpu.VMEM((2, 128, X), WIDE),
            pltpu.VMEM((NX // 2, ROWS, X), WIDE),
            pltpu.VMEM((OWNERS, ROWS, 128), HALF),
            pltpu.VMEM((NT, ROWS, 128), HALF),
            pltpu.VMEM((OWNERS, ROWS, 128), HALF),
            dma((7,)), dma((31,)), dma((len(BATCH),)), dma((len(BATCH),)), dma((len(BATCH),)),
            dma, dma, dma, dma, dma, dma, dma, dma((OWNERS,)), dma((OWNERS,)), dma, dma,
        ],
        compiler_params=pltpu.CompilerParams(
            collective_id=0, has_side_effects=True, vmem_limit_bytes=56 * 1024 * 1024
        ),
        cost_estimate=pl.CostEstimate(flops=2_500_000_000, bytes_accessed=6_000_000, transcendentals=0),
        name="interaction_backward",
    )(x, g, lengths, w_lcb, projection, w_fmb, feature_order.reshape(1, F), col_layout.T)
    out, lcb, fmb, proj = pl.pallas_call(
        place,
        out_shape=(
            jax.ShapeDtypeStruct((X, 512), WIDE),
            jax.ShapeDtypeStruct((F, F), WIDE),
            jax.ShapeDtypeStruct((K, D), WIDE),
            jax.ShapeDtypeStruct((K, F), WIDE),
        ),
        in_specs=[hbm] * 2,
        out_specs=(hbm,) * 4,
        scratch_shapes=[
            pltpu.VMEM((512, X), HALF),
            pltpu.VMEM((NX, OWNERS, ROWS, 128), HALF),
            pltpu.VMEM((X, 512), WIDE),
            pltpu.VMEM((F, F), WIDE),
            pltpu.VMEM((K, D), WIDE),
            pltpu.VMEM((K, F), WIDE),
            dma((2,)), dma((4,)),
        ],
        compiler_params=pltpu.CompilerParams(vmem_limit_bytes=56 * 1024 * 1024),
        name="place",
    )(rows.reshape(512, X), full)
    return out.reshape(ROWS, PIECE, 512).transpose(0, 2, 1), lcb, fmb, proj


def solution(mesh):
    placed = P(("table", "col", "rep"), None, None)
    return jax.shard_map(
        body,
        mesh=mesh,
        in_specs=(placed, placed, P(("table", "col", "rep"), None), P(), P(), P(), P(), P()),
        out_specs=(P("table", "rep", "col"), P(), P(), P()),
        check_vma=False,
    )
```
